32 devices in a mesh: parts: 2 (over x), node: 16 (over z, y, core).
Axes of the slice: x: 2, y: 2, z: 4, core: 2. Of those that a mesh axis runs over, the one named last changes fastest.
Arguments:
- node_field: float32 [64, 8192], P(None, ('parts', 'node')), parts along dimension 1, may hold values from -8 to 8
- first_messages: float32 [64, 65536], P(None, ('parts', 'node')), parts along dimension 1, may hold values from 0.05 to 1
- affinity: float32 [64, 64], replicated, may hold values from 1 to 30, as said below
- group_share: float32 [64], replicated, may hold values from 0.005 to 0.05
- dst_node: int32 [65536], P(('parts', 'node')), parts along dimension 0, may hold values from 0 to 256, as said below
- send_slots: int32 [32768], P(('parts', 'node')), parts along dimension 0, may hold values from 0 to 2047, as said below
- source_slot: int32 [65536], P(('parts', 'node')), parts along dimension 0, may hold values from 0 to 3071, as said below
Outputs:
- marginals: float32 [64, 8192], P(None, ('parts', 'node')), parts along dimension 1
- cavity_terms: float32 [64, 65536], P(None, ('parts', 'node')), parts along dimension 1
The draws below stay inside these ranges and needn't reach their ends.
There are 2 independent parts, one for each index of `parts`. The reference program is written for one: setup_inputs(seed, part) draws one part's arguments, and reference() takes and returns one part's arrays. A program takes and returns all parts, laid end to end along the dimension named above; an argument that names none is the same for every part. Nothing has to cross between parts.
Inputs may be any that keep to these rules, and one draw needn't show every extreme that they name: `dst_node`: on each device the 2048 slots list the live edges by receiving node, sorted, then the padding marked 256; every device has a node with 96 or more incoming edges. `send_slots`: entry b * 64 + t of a device's 16 * 64 entries is the slot whose new message travels to device b into place t; at most 64 of the entries for one peer are live slots, and every device has exactly 64 live ones for one peer, also in the other direction. `source_slot`: each live slot names the live slot of its reverse edge, among this device's 2048 slots or among the 1024 places received; a padding slot names itself. `affinity`: Symmetric.
All inputs are finite; a program needn't handle non-finite values.
Results may differ from the reference program's by a relative error of at most 0.0003.
Values sent between devices are 32-bit elements; how exact they have to be, the bound alone decides.
A program may use at most 64 MiB of HBM per device.

```python
import math
import jax
import jax.numpy as jnp
from jax import lax

GROUPS = 64
CAP = 64
NODE_DEV = 256
HUB = 96
ROUNDS = 2
SWEEPS = 2
E_DEV = 2048
SLOTS = 32768
NODES = 4096
N_NODE = 16


def build_graph(key):
    subkeys = jax.random.split(key, 6)
    region = N_NODE * CAP
    device_ids = jnp.arange(N_NODE, dtype=jnp.int32)
    pairing = jax.random.permutation(subkeys[0], N_NODE).astype(jnp.int32)
    slot_rank = jnp.argsort(pairing).astype(jnp.int32)
    partner = pairing[slot_rank ^ 1]
    counts_raw = jax.random.randint(subkeys[1], (N_NODE, N_NODE), 1, CAP + 1)
    counts = jnp.minimum((counts_raw + counts_raw.T) // 2, CAP - 1)
    counts = jnp.where(partner[:, None] == device_ids[None, :], CAP, counts)
    counts = jnp.where(device_ids[:, None] == device_ids[None, :], 0, counts)
    logical = jnp.arange(E_DEV, dtype=jnp.int32)
    peer_of = jnp.minimum(logical // CAP, N_NODE - 1)
    within = logical % CAP
    live_log = jnp.where(logical[None, :] < region, within[None, :] < counts[:, peer_of], True)
    shuffle = jax.vmap(lambda kk: jax.random.permutation(kk, E_DEV))(jax.random.split(subkeys[2], N_NODE)).astype(jnp.int32)
    order_score = jnp.where(live_log, 0, E_DEV) + shuffle
    phys_to_log = jnp.argsort(order_score, axis=1).astype(jnp.int32)
    log_to_phys = jnp.argsort(phys_to_log, axis=1).astype(jnp.int32)
    live_count = jnp.sum(live_log.astype(jnp.int32), axis=1)
    first_draw = jax.random.randint(subkeys[3], (N_NODE, E_DEV), 0, NODE_DEV - 1)
    second = jax.random.randint(subkeys[4], (N_NODE, E_DEV), 0, NODE_DEV - 1)
    raw_node = jnp.where(logical[None, :] < HUB, 0, 1 + jnp.minimum(first_draw, second)).astype(jnp.int32)
    relabel = jax.vmap(lambda kk: jax.random.permutation(kk, NODE_DEV))(jax.random.split(subkeys[5], N_NODE)).astype(jnp.int32)
    mapped = jnp.take_along_axis(relabel, raw_node, axis=1)
    mapped = jnp.where(logical[None, :] < live_count[:, None], mapped, NODE_DEV)
    dst_table = jnp.sort(mapped, axis=1).astype(jnp.int32)
    send_table = log_to_phys[:, :region]
    partner_log = jnp.clip(region + (phys_to_log - region ^ 1), 0, E_DEV - 1)
    local_source = jnp.take_along_axis(log_to_phys, partner_log, axis=1)
    live_phys = jnp.take_along_axis(live_log, phys_to_log, axis=1)
    source_table = jnp.where(phys_to_log < region, E_DEV + phys_to_log, local_source)
    source_table = jnp.where(live_phys, source_table, logical[None, :]).astype(jnp.int32)
    return (dst_table.reshape(-1), send_table.reshape(-1), source_table.reshape(-1))


def draw_dst_node(key, part):
    return build_graph(key)[0]


def draw_send_slots(key, part):
    return build_graph(key)[1]


def draw_source_slot(key, part):
    return build_graph(key)[2]


def draw_affinity(key, part):
    key = jax.random.fold_in(key, 11)
    base_draw = jnp.exp(jax.random.uniform(key, (GROUPS, GROUPS), jnp.float32, 0.0, math.log(30.0)))
    return 0.5 * (base_draw + base_draw.T)


def raised(values, stream_key, source, target, blocks, factor):
    owner, partner = [(jnp.arange(values.shape[axis_at]) // (values.shape[axis_at] // blocks)).reshape([-1 if axis == axis_at else 1 for axis in range(values.ndim)]) for axis_at in (source, target)]
    chosen = jax.random.permutation(stream_key, blocks)[partner]
    strong = (owner == chosen) | (owner == (partner + blocks // 2) % blocks)
    return jnp.where(strong, factor * values, values)


def level_of(rng, shape, cuts, least, high):
    def one(position, shards_of):
        draws = jax.random.uniform(jax.random.fold_in(jax.random.fold_in(rng, 6), position), (shards_of,), jnp.float32, least / len(cuts), high / len(cuts))
        return jnp.repeat(jnp.exp(draws), shape[position] // shards_of).reshape((-1,) + (1,) * (len(shape) - position - 1))

    factor_of = one(*cuts[0])
    for cut in cuts[1:]:
        factor_of = factor_of * one(*cut)
    return factor_of


def noise_with(stream_key, dims, spread, limit, cuts, heavy, kind=jnp.bfloat16):
    result = spread * jax.random.normal(stream_key, dims, jnp.float32)
    if cuts:
        result = result * level_of(stream_key, dims, cuts, -0.22, 0.18)
    return jnp.clip(raised(result, jax.random.fold_in(stream_key, 3), *heavy), -limit, limit).astype(kind)


def setup_inputs(seed: int = 0, part: int = 0) -> dict:
    keys = jax.random.split(jax.random.key(seed), 8)
    part_keys = jax.random.split(jax.random.fold_in(keys[7], part), 8)
    node_field = noise_with(part_keys[0], (GROUPS, NODES), 1.0, 8.0, ((1, 16),), (1, 0, 16, 2.0), jnp.float32)
    first_messages = jnp.clip(jnp.exp(math.log(1.0) - 2.9957323 * jax.random.uniform(part_keys[1], (GROUPS, SLOTS), jnp.float32) ** level_of(part_keys[1], (GROUPS, SLOTS), ((1, 16),), -0.2, 0.2)), 0.05, 1.0)
    affinity = draw_affinity(jax.random.fold_in(keys[7], 71), part)
    group_share = jnp.clip(jnp.exp(jax.random.uniform(keys[3], (GROUPS,), jnp.float32, math.log(0.005), math.log(0.05))), 0.005, 0.05)
    dst_node = draw_dst_node(jax.random.fold_in(jax.random.fold_in(keys[7], part), 71), part)
    send_slots = draw_send_slots(jax.random.fold_in(jax.random.fold_in(keys[7], part), 71), part)
    source_slot = draw_source_slot(jax.random.fold_in(jax.random.fold_in(keys[7], part), 71), part)
    return {"node_field": node_field, "first_messages": first_messages, "affinity": affinity, "group_share": group_share, "dst_node": dst_node, "send_slots": send_slots, "source_slot": source_slot}


def softmax_groups(logits):
    largest = jnp.max(logits, axis=0, keepdims=True)
    weights = jnp.exp(logits - largest)
    return weights / jnp.sum(weights, axis=0, keepdims=True)


def masked_logs(affinity, messages, in_use):
    flat = messages.reshape(messages.shape[0], -1)
    product = jnp.dot(affinity, flat, precision=lax.Precision.HIGHEST, preferred_element_type=jnp.float32)
    product = product.reshape(messages.shape)
    return jnp.log(jnp.where(in_use[None], product, 1.0))


def reference(node_field, first_messages, affinity, group_share, dst_node, send_slots, source_slot):
    device_count = N_NODE
    dst_table = dst_node.reshape(device_count, E_DEV)
    in_use = dst_table < NODE_DEV
    clipped = jnp.minimum(dst_table, NODE_DEV - 1)
    send_rows = send_slots.reshape(device_count, device_count * CAP)
    source_table = source_slot.reshape(device_count, E_DEV)
    device_row = jnp.broadcast_to(jnp.arange(device_count, dtype=jnp.int32)[:, None], (device_count, E_DEV))
    device_send = jnp.broadcast_to(jnp.arange(device_count, dtype=jnp.int32)[:, None], (device_count, device_count * CAP))
    evidence = node_field.reshape(GROUPS, device_count, NODE_DEV)
    base_field = jnp.log(group_share)[:, None, None] + evidence

    def node_sums(cavity):
        totals = jnp.zeros((GROUPS, device_count, NODE_DEV + 1), jnp.float32)
        totals = totals.at[:, device_row, dst_table].add(cavity)
        return totals[:, :, :NODE_DEV]

    cavity = masked_logs(affinity, first_messages.reshape(GROUPS, device_count, E_DEV), in_use)
    totals = node_sums(cavity)
    node_base = base_field
    for round_index in range(ROUNDS):
        belief = softmax_groups(base_field + totals)
        group_mass = jnp.sum(belief, axis=(1, 2))
        field_shift = jnp.dot(affinity, group_mass, precision=lax.Precision.HIGHEST, preferred_element_type=jnp.float32) / (NODE_DEV * device_count)
        node_base = base_field - field_shift[:, None, None]
        for sweep_index in range(SWEEPS):
            node_logit = node_base + totals
            outgoing = softmax_groups(node_logit[:, device_row, clipped] - cavity)
            outbound = outgoing[:, device_send, send_rows].reshape(GROUPS, device_count, device_count, CAP)
            received = jnp.transpose(outbound, (0, 2, 1, 3)).reshape(GROUPS, device_count, device_count * CAP)
            candidates = jnp.concatenate([outgoing, received], axis=2)
            renewed = jnp.take_along_axis(candidates, source_table[None], axis=2)
            renewed = jnp.where(in_use[None], renewed, 0.0)
            cavity = masked_logs(affinity, renewed, in_use)
            totals = node_sums(cavity)
    marginals = softmax_groups(node_base + totals)
    return marginals.reshape(GROUPS, -1), cavity.reshape(GROUPS, -1)
```

```python
import functools

import jax
import jax.numpy as jnp
from jax import lax
from jax.experimental import pallas as pl
from jax.experimental.pallas import tpu as pltpu
from jax.sharding import PartitionSpec as P

ROUNDS = 2
SWEEPS = 2
TILE = 256
F32 = jnp.float32
BF16 = jnp.bfloat16
LAST = (((1,), (1,)), ((), ()))


def split_three(x):
    high = x.astype(BF16)
    rest = x - high.astype(F32)
    middle = rest.astype(BF16)
    low = (rest - middle.astype(F32)).astype(BF16)
    return jnp.concatenate([high, middle, low], axis=0)


def join_three(x):
    g = x.shape[0] // 3
    return x[:g] + x[g : 2 * g] + x[2 * g :]


def softmax_groups(logits):
    weights = jnp.exp(logits - jnp.max(logits, axis=0, keepdims=True))
    return weights / jnp.sum(weights, axis=0, keepdims=True)


def loop(count, body, init):
    return lax.fori_loop(0, count, body, init, unroll=count <= 4)


def kernel(
    n, field_ref, first_ref, aff_ref, share_ref, dst_ref, send_ref, own_ref, src_ref,
    marg_ref, out_ref,
    vals, cav, member, live, chosen, pos_ref, partner, sbuf, rbuf, mass_out, mass_in,
    send_sem, recv_sem, msend_sem, mrecv_sem,
):
    me = lax.axis_index("node")
    groups, nodes = field_ref.shape
    slots = first_ref.shape[1]
    places = send_ref.shape[1]
    cap = places // n
    pairs = slots // 2
    width = 512
    every_node = nodes * n

    barrier = pltpu.get_barrier_semaphore()

    @pl.loop(1, n)
    def _(i):
        pl.semaphore_signal(
            barrier, inc=1, device_id={"node": lax.rem(me + i, n)},
            device_id_type=pl.DeviceIdType.MESH,
        )

    aff = aff_ref[...]
    aff_high = aff.astype(BF16)
    aff_mid = (aff - aff_high.astype(F32)).astype(BF16)
    aff_wide = jnp.concatenate([aff_high, aff_high, aff_mid, aff_mid], axis=1)

    def group_logs(messages, alive):
        high = messages.astype(BF16)
        mid = (messages - high.astype(F32)).astype(BF16)
        stacked = jnp.concatenate([high, mid, high, mid], axis=0)
        product = jnp.dot(aff_wide, stacked, preferred_element_type=F32)
        return jnp.log(jnp.where(alive, product, 1.0))

    dst = dst_ref[...]
    src = src_ref[...]
    in_use = dst < nodes
    own = own_ref[pl.ds(me, 1), :]
    row16 = lax.broadcasted_iota(jnp.int32, (16, cap), 0)
    own_digits = jnp.where(row16 == 0, own >> 6, own & 63).astype(F32).astype(BF16)
    own_hot = jnp.where(
        lax.broadcasted_iota(jnp.int32, (cap, slots), 0) == src - (slots + me * cap), 1.0, 0.0
    ).astype(BF16)
    own_slot = jnp.dot(own_digits, own_hot, preferred_element_type=F32)
    own_slot = (own_slot[0:1] * 64.0 + own_slot[1:2]).astype(jnp.int32)
    through_own = (src >= slots + me * cap) & (src < slots + (me + 1) * cap)
    src = jnp.where(through_own, own_slot, src)
    slot_id = lax.broadcasted_iota(jnp.int32, (1, slots), 1)
    leads = in_use & (src < slots) & (src > slot_id)
    lead_f = jnp.where(leads, 1.0, 0.0)
    before = jnp.where(
        lax.broadcasted_iota(jnp.int32, (TILE, TILE), 0)
        < lax.broadcasted_iota(jnp.int32, (TILE, TILE), 1), 1.0, 0.0,
    ).astype(BF16)
    carry = jnp.zeros((1, 1), F32)
    ranks = []
    for c in range(slots // TILE):
        piece = lead_f[:, c * TILE : (c + 1) * TILE]
        inner = jnp.dot(
            jnp.broadcast_to(piece, (16, TILE)).astype(BF16), before, preferred_element_type=F32
        )[0:1]
        ranks.append(inner + carry)
        carry = carry + jnp.sum(piece, axis=1, keepdims=True)
    rank = jnp.concatenate(ranks, axis=1).astype(jnp.int32)
    position = jnp.where(
        leads, places + rank, jnp.where(in_use & (src >= slots), src - slots, -1)
    )
    pos_ref[...] = jnp.broadcast_to(position, pos_ref.shape)

    row = lax.broadcasted_iota(jnp.int32, (16, slots), 0)
    src1 = src + 1
    slot1 = slot_id + 1
    digits = jnp.where(
        row == 0, dst + 1,
        jnp.where(
            row == 1, src1 >> 6,
            jnp.where(row == 2, src1 & 63, jnp.where(row == 3, slot1 >> 6, slot1 & 63)),
        ),
    )
    vals[3 * groups :, :] = digits.astype(F32).astype(BF16)

    def start_logs(c, _):
        cols = pl.ds(pl.multiple_of(c * width, width), width)
        vals[: 3 * groups, cols] = split_three(
            group_logs(first_ref[:, cols], dst_ref[:, cols] < nodes)
        )
        return 0

    loop(slots // width, start_logs, 0)

    node_id = lax.broadcasted_iota(jnp.int32, (nodes, TILE), 0)

    def keep(cols, moved):
        cav[:, cols] = join_three(moved[: 3 * groups])
        node1 = moved[3 * groups : 3 * groups + 1].astype(jnp.int32)
        member[:, cols] = jnp.where(node_id + 1 == node1, 1.0, 0.0).astype(BF16)
        live[:, cols] = jnp.broadcast_to(node1, (8, TILE))

    def to_slot(start):
        ids = lax.broadcasted_iota(jnp.int32, (TILE, slots), 0) + start
        return jnp.where(ids == pos_ref[0:1, :], 1.0, 0.0).astype(BF16)

    def from_partner(c):
        cols = pl.ds(pl.multiple_of(c * TILE, TILE), TILE)
        ids = lax.broadcasted_iota(jnp.int32, (slots, TILE), 0)
        return jnp.where(ids == partner[0:1, cols], 1.0, 0.0).astype(BF16)

    def place_received(c, _):
        start = pl.multiple_of(c * TILE, TILE)
        hot = to_slot(start)
        keep(pl.ds(start, TILE), lax.dot_general(vals[...], hot, LAST, preferred_element_type=F32))
        held = lax.dot_general(hot, vals[3 * groups :, :], LAST, preferred_element_type=F32)
        held = (held[:, 3:4] * 64.0 + held[:, 4:5]).astype(jnp.int32) - 1
        chosen[c] = jnp.where(held == send_ref[:, pl.ds(start, TILE)], 1.0, 0.0).astype(BF16)
        return 0

    lax.fori_loop(0, places // TILE, place_received, 0)

    def place_pairs(c, _):
        start = pl.multiple_of(places + c * TILE, TILE)
        moved = lax.dot_general(vals[...], to_slot(start), LAST, preferred_element_type=F32)
        keep(pl.ds(start, TILE), moved)
        other = moved[3 * groups + 1 : 3 * groups + 2] * 64.0 + moved[3 * groups + 2 : 3 * groups + 3]
        cols = pl.ds(pl.multiple_of(c * TILE, TILE), TILE)
        partner[:, cols] = jnp.broadcast_to(other.astype(jnp.int32) - 1, (8, TILE))
        moved = jnp.dot(vals[...], from_partner(c), preferred_element_type=F32)
        keep(pl.ds(pl.multiple_of(start + pairs, TILE), TILE), moved)
        return 0

    lax.fori_loop(0, pairs // TILE, place_pairs, 0)

    for step in range(ROUNDS * SWEEPS):
        rbuf[step, me] = jnp.zeros(rbuf.shape[2:], F32)

    def add_up(acc, cols, terms):
        return acc + lax.dot_general(
            split_three(terms), member[:, cols], LAST, preferred_element_type=F32
        )

    def sum_start(c, acc):
        cols = pl.ds(pl.multiple_of(c * width, width), width)
        return add_up(acc, cols, cav[:, cols])

    zero = jnp.zeros((3 * groups, nodes), F32)
    totals = join_three(loop((places + slots) // width, sum_start, zero))
    base = jnp.log(share_ref[...]) + field_ref[...]
    half = lax.broadcasted_iota(jnp.int32, (groups // 2, 2 * cap), 1) < cap
    pl.semaphore_wait(barrier, n - 1)

    node_base = base
    weight = jnp.ones((groups, 1), F32)
    for round_index in range(ROUNDS):
        for sweep_index in range(SWEEPS):
            step = round_index * SWEEPS + sweep_index
            late = sweep_index == 0
            if late:
                belief = softmax_groups(base + totals)
                mass = lax.dot_general(
                    jnp.ones((8, nodes), BF16), split_three(belief), LAST,
                    preferred_element_type=F32,
                )
                mass = mass[:, :groups] + mass[:, groups : 2 * groups] + mass[:, 2 * groups :]
                mass = jnp.concatenate([mass, jnp.zeros_like(mass)], axis=1)
                mass_out[round_index] = mass
                mass_in[round_index, me] = mass

                @pl.loop(1, n)
                def _(i):
                    pltpu.make_async_remote_copy(
                        src_ref=mass_out.at[round_index], dst_ref=mass_in.at[round_index, me],
                        send_sem=msend_sem.at[round_index], recv_sem=mrecv_sem.at[round_index],
                        device_id={"node": lax.rem(me + i, n)},
                        device_id_type=pl.DeviceIdType.MESH,
                    ).start()

            logit = (base if late else node_base) + totals
            logit = split_three(logit - jnp.max(logit, axis=0, keepdims=True))

            def outgoing(cols):
                at_slot = join_three(jnp.dot(logit, member[:, cols], preferred_element_type=F32))
                at_slot = at_slot - cav[:, cols]
                return jnp.exp(at_slot - jnp.max(at_slot, axis=0, keepdims=True))

            def send_part(c, _):
                start = pl.multiple_of(c * TILE, TILE)
                out = outgoing(pl.ds(start, TILE))
                out = join_three(
                    jnp.dot(split_three(out), chosen[c], preferred_element_type=F32)
                )
                for j in range(TILE // (2 * cap)):
                    x = out[:, j * 2 * cap : (j + 1) * 2 * cap]
                    r = pltpu.roll(x, cap, 1)
                    peer = c * (TILE // cap) + 2 * j
                    sbuf[step, peer] = jnp.where(half, x[: groups // 2], r[groups // 2 :])
                    sbuf[step, peer + 1] = jnp.where(half, r[: groups // 2], x[groups // 2 :])
                return 0

            loop(places // TILE, send_part, 0)

            @pl.loop(1, n)
            def _(i):
                peer = lax.rem(me + i, n)
                pltpu.make_async_remote_copy(
                    src_ref=sbuf.at[step, peer], dst_ref=rbuf.at[step, me],
                    send_sem=send_sem.at[step], recv_sem=recv_sem.at[step],
                    device_id={"node": peer}, device_id_type=pl.DeviceIdType.MESH,
                ).start()

            if late:
                arrived = mass_in.at[round_index, pl.ds(0, n - 1)]
                pltpu.make_async_copy(arrived, arrived, mrecv_sem.at[round_index]).wait()
                mass = loop(
                    n, lambda b, acc: acc + mass_in[round_index, b], jnp.zeros((8, 2 * cap), F32)
                )
                shift = jnp.sum(aff * mass[0:1, :groups], axis=1, keepdims=True) / every_node
                node_base = base - shift
                weight = jnp.exp(jnp.min(shift, axis=0, keepdims=True) - shift)

            def renew(cols, messages):
                messages = messages * weight
                scale = jnp.maximum(jnp.sum(messages, axis=0, keepdims=True), 1e-30)
                return group_logs(messages / scale, live[0:1, cols] > 0)

            if not late:
                weight = jnp.ones((groups, 1), F32)

            def local_part(c, acc):
                lead = pl.ds(pl.multiple_of(places + c * width, width), width)
                back = pl.ds(pl.multiple_of(places + pairs + c * width, width), width)
                lead_out, back_out = outgoing(lead), outgoing(back)
                lead_new, back_new = renew(lead, back_out), renew(back, lead_out)
                cav[:, lead] = lead_new
                cav[:, back] = back_new
                return add_up(add_up(acc, lead, lead_new), back, back_new)

            acc = loop(pairs // width, local_part, zero)

            arrived = rbuf.at[step, pl.ds(0, n - 1)]
            pltpu.make_async_copy(arrived, arrived, recv_sem.at[step]).wait()

            def take_part(c, acc):
                cols = pl.ds(pl.multiple_of(c * width, width), width)
                tiles = []
                for j in range(width // (2 * cap)):
                    peer = c * (width // cap) + 2 * j
                    b0, b1 = rbuf[step, peer], rbuf[step, peer + 1]
                    top = jnp.where(half, b0, pltpu.roll(b1, cap, 1))
                    low = jnp.where(half, pltpu.roll(b0, cap, 1), b1)
                    tiles.append(jnp.concatenate([top, low], axis=0))
                fresh = renew(cols, jnp.concatenate(tiles, axis=1))
                cav[:, cols] = fresh
                return add_up(acc, cols, fresh)

            totals = join_three(loop(places // width, take_part, acc))

    marg_ref[...] = softmax_groups(node_base + totals)

    out_ref[...] = jnp.zeros_like(out_ref)

    def back_first(c, _):
        start = pl.multiple_of(c * TILE, TILE)
        terms = split_three(cav[:, pl.ds(start, TILE)])
        out_ref[...] += join_three(jnp.dot(terms, to_slot(start), preferred_element_type=F32))
        return 0

    lax.fori_loop(0, (places + pairs) // TILE, back_first, 0)

    def back_partner(c, _):
        start = pl.multiple_of(places + pairs + c * TILE, TILE)
        terms = split_three(cav[:, pl.ds(start, TILE)])
        out_ref[...] += join_three(
            lax.dot_general(terms, from_partner(c), LAST, preferred_element_type=F32)
        )
        return 0

    lax.fori_loop(0, pairs // TILE, back_partner, 0)

    for step in range(ROUNDS * SWEEPS):
        sent = sbuf.at[step, pl.ds(0, n - 1)]
        pltpu.make_async_copy(sent, sent, send_sem.at[step]).wait()
    for round_index in range(ROUNDS):
        sent = mass_in.at[round_index, pl.ds(0, n - 1)]
        pltpu.make_async_copy(sent, sent, msend_sem.at[round_index]).wait()


def on_device(node_field, first_messages, affinity, group_share, dst_node, send_slots, source_slot):
    n = lax.axis_size("node")
    groups, nodes = node_field.shape
    slots = first_messages.shape[1]
    places = send_slots.shape[0]
    cap = places // n
    steps = ROUNDS * SWEEPS
    total = places + slots
    vmem = pl.BlockSpec(memory_space=pltpu.VMEM)
    return pl.pallas_call(
        functools.partial(kernel, n),
        out_shape=(
            jax.ShapeDtypeStruct((groups, nodes), F32),
            jax.ShapeDtypeStruct((groups, slots), F32),
        ),
        in_specs=[vmem] * 8,
        out_specs=(vmem, vmem),
        scratch_shapes=[
            pltpu.VMEM((3 * groups + 16, slots), BF16),
            pltpu.VMEM((groups, total), F32),
            pltpu.VMEM((nodes, total), BF16),
            pltpu.VMEM((8, total), jnp.int32),
            pltpu.VMEM((places // TILE, TILE, TILE), BF16),
            pltpu.VMEM((8, slots), jnp.int32),
            pltpu.VMEM((8, slots // 2), jnp.int32),
            pltpu.VMEM((steps, n, groups // 2, 2 * cap), F32),
            pltpu.VMEM((steps, n, groups // 2, 2 * cap), F32),
            pltpu.VMEM((ROUNDS, 8, 2 * cap), F32),
            pltpu.VMEM((ROUNDS, n, 8, 2 * cap), F32),
            pltpu.SemaphoreType.DMA((steps,)),
            pltpu.SemaphoreType.DMA((steps,)),
            pltpu.SemaphoreType.DMA((ROUNDS,)),
            pltpu.SemaphoreType.DMA((ROUNDS,)),
        ],
        compiler_params=pltpu.CompilerParams(
            collective_id=0, has_side_effects=True, vmem_limit_bytes=52 * 1024 * 1024
        ),
    )(
        node_field,
        first_messages,
        affinity,
        group_share.reshape(groups, 1),
        dst_node.reshape(1, slots),
        send_slots.reshape(1, places),
        send_slots.reshape(n, cap),
        source_slot.reshape(1, slots),
    )


def solution(mesh):
    split = P(None, ("parts", "node"))
    flat = P(("parts", "node"))
    return jax.shard_map(
        on_device,
        mesh=mesh,
        in_specs=(split, split, P(), P(), flat, flat, flat),
        out_specs=(split, split),
        check_vma=False,
    )
```

```python
import functools

import jax
import jax.numpy as jnp
from jax import lax
from jax.experimental import pallas as pl
from jax.experimental.pallas import tpu as pltpu
from jax.sharding import PartitionSpec as P

ROUNDS = 2
SWEEPS = 2
TILE = 256
F32 = jnp.float32
BF16 = jnp.bfloat16
LAST = (((1,), (1,)), ((), ()))


def split_three(x):
    high = x.astype(BF16)
    rest = x - high.astype(F32)
    middle = rest.astype(BF16)
    low = (rest - middle.astype(F32)).astype(BF16)
    return jnp.concatenate([high, middle, low], axis=0)


def join_three(x):
    g = x.shape[0] // 3
    return x[:g] + x[g : 2 * g] + x[2 * g :]


def softmax_groups(logits):
    weights = jnp.exp(logits - jnp.max(logits, axis=0, keepdims=True))
    return weights / jnp.sum(weights, axis=0, keepdims=True)


def loop(count, body, init):
    return lax.fori_loop(0, count, body, init, unroll=count <= 4)


def kernel(
    n, field_ref, first_ref, aff_ref, share_ref, dst_ref, send_ref, own_ref, src_ref,
    marg_ref, out_ref,
    vals, cav, member, live, chosen, pos_ref, partner, sbuf, rbuf, mass_out, mass_in,
    send_sem, recv_sem, msend_sem, mrecv_sem,
):
    me = lax.axis_index("node")
    groups, nodes = field_ref.shape
    slots = first_ref.shape[1]
    places = send_ref.shape[1]
    cap = places // n
    pairs = slots // 2
    width = 512
    planes = places // TILE
    group = TILE // cap
    plane = me // group
    far_first = sorted(range(planes), key=lambda o: (-min(o, planes - o), o))
    every_node = nodes * n

    barrier = pltpu.get_barrier_semaphore()

    @pl.loop(1, n)
    def _(i):
        pl.semaphore_signal(
            barrier, inc=1, device_id={"node": lax.rem(me + i, n)},
            device_id_type=pl.DeviceIdType.MESH,
        )

    aff = aff_ref[...]
    aff_high = aff.astype(BF16)
    aff_mid = (aff - aff_high.astype(F32)).astype(BF16)
    aff_wide = jnp.concatenate([aff_high, aff_high, aff_mid, aff_mid], axis=1)

    def group_logs(messages, alive):
        high = messages.astype(BF16)
        mid = (messages - high.astype(F32)).astype(BF16)
        stacked = jnp.concatenate([high, mid, high, mid], axis=0)
        product = jnp.dot(aff_wide, stacked, preferred_element_type=F32)
        return jnp.log(jnp.where(alive, product, 1.0))

    dst = dst_ref[...]
    src = src_ref[...]
    in_use = dst < nodes
    own = own_ref[pl.ds(me, 1), :]
    row16 = lax.broadcasted_iota(jnp.int32, (16, cap), 0)
    own_digits = jnp.where(row16 == 0, own >> 6, own & 63).astype(F32).astype(BF16)
    own_hot = jnp.where(
        lax.broadcasted_iota(jnp.int32, (cap, slots), 0) == src - (slots + me * cap), 1.0, 0.0
    ).astype(BF16)
    own_slot = jnp.dot(own_digits, own_hot, preferred_element_type=F32)
    own_slot = (own_slot[0:1] * 64.0 + own_slot[1:2]).astype(jnp.int32)
    through_own = (src >= slots + me * cap) & (src < slots + (me + 1) * cap)
    src = jnp.where(through_own, own_slot, src)
    slot_id = lax.broadcasted_iota(jnp.int32, (1, slots), 1)
    leads = in_use & (src < slots) & (src > slot_id)
    lead_f = jnp.where(leads, 1.0, 0.0)
    before = jnp.where(
        lax.broadcasted_iota(jnp.int32, (TILE, TILE), 0)
        < lax.broadcasted_iota(jnp.int32, (TILE, TILE), 1), 1.0, 0.0,
    ).astype(BF16)
    carry = jnp.zeros((1, 1), F32)
    ranks = []
    for c in range(slots // TILE):
        piece = lead_f[:, c * TILE : (c + 1) * TILE]
        inner = jnp.dot(
            jnp.broadcast_to(piece, (16, TILE)).astype(BF16), before, preferred_element_type=F32
        )[0:1]
        ranks.append(inner + carry)
        carry = carry + jnp.sum(piece, axis=1, keepdims=True)
    rank = jnp.concatenate(ranks, axis=1).astype(jnp.int32)
    position = jnp.where(
        leads, places + rank, jnp.where(in_use & (src >= slots), src - slots, -1)
    )
    pos_ref[...] = jnp.broadcast_to(position, pos_ref.shape)

    row = lax.broadcasted_iota(jnp.int32, (16, slots), 0)
    src1 = src + 1
    slot1 = slot_id + 1
    digits = jnp.where(
        row == 0, dst + 1,
        jnp.where(
            row == 1, src1 >> 6,
            jnp.where(row == 2, src1 & 63, jnp.where(row == 3, slot1 >> 6, slot1 & 63)),
        ),
    )
    vals[3 * groups :, :] = digits.astype(F32).astype(BF16)

    zero = jnp.zeros((3 * groups, nodes), F32)

    def start_logs(c, acc):
        cols = pl.ds(pl.multiple_of(c * width, width), width)
        terms = split_three(group_logs(first_ref[:, cols], dst_ref[:, cols] < nodes))
        vals[: 3 * groups, cols] = terms
        ids = lax.broadcasted_iota(jnp.int32, (nodes, width), 0)
        hot = jnp.where(ids == dst_ref[:, cols], 1.0, 0.0).astype(BF16)
        return acc + lax.dot_general(terms, hot, LAST, preferred_element_type=F32)

    totals = join_three(loop(slots // width, start_logs, zero))

    node_id = lax.broadcasted_iota(jnp.int32, (nodes, TILE), 0)

    def keep(cols, moved):
        cav[:, cols] = join_three(moved[: 3 * groups])
        node1 = moved[3 * groups : 3 * groups + 1].astype(jnp.int32)
        member[:, cols] = jnp.where(node_id + 1 == node1, 1.0, 0.0).astype(BF16)
        live[:, cols] = jnp.broadcast_to(node1, (8, TILE))

    def to_slot(start):
        ids = lax.broadcasted_iota(jnp.int32, (TILE, slots), 0) + start
        return jnp.where(ids == pos_ref[0:1, :], 1.0, 0.0).astype(BF16)

    def from_partner(c):
        cols = pl.ds(pl.multiple_of(c * TILE, TILE), TILE)
        ids = lax.broadcasted_iota(jnp.int32, (slots, TILE), 0)
        return jnp.where(ids == partner[0:1, cols], 1.0, 0.0).astype(BF16)

    def place_received(c, _):
        start = pl.multiple_of(c * TILE, TILE)
        hot = to_slot(start)
        keep(pl.ds(start, TILE), lax.dot_general(vals[...], hot, LAST, preferred_element_type=F32))
        held = lax.dot_general(hot, vals[3 * groups :, :], LAST, preferred_element_type=F32)
        held = (held[:, 3:4] * 64.0 + held[:, 4:5]).astype(jnp.int32) - 1
        chosen[c] = jnp.where(held == send_ref[:, pl.ds(start, TILE)], 1.0, 0.0).astype(BF16)
        return 0

    lax.fori_loop(0, places // TILE, place_received, 0)

    def place_pairs(c, _):
        start = pl.multiple_of(places + c * TILE, TILE)
        moved = lax.dot_general(vals[...], to_slot(start), LAST, preferred_element_type=F32)
        keep(pl.ds(start, TILE), moved)
        other = moved[3 * groups + 1 : 3 * groups + 2] * 64.0 + moved[3 * groups + 2 : 3 * groups + 3]
        cols = pl.ds(pl.multiple_of(c * TILE, TILE), TILE)
        partner[:, cols] = jnp.broadcast_to(other.astype(jnp.int32) - 1, (8, TILE))
        moved = jnp.dot(vals[...], from_partner(c), preferred_element_type=F32)
        keep(pl.ds(pl.multiple_of(start + pairs, TILE), TILE), moved)
        return 0

    for step in range(ROUNDS * SWEEPS):
        rbuf[step, me] = jnp.zeros(rbuf.shape[2:], F32)

    def add_up(acc, cols, terms):
        return acc + lax.dot_general(
            split_three(terms), member[:, cols], LAST, preferred_element_type=F32
        )

    square = (groups, groups)
    diagonal = lax.broadcasted_iota(jnp.int32, square, 0) == lax.broadcasted_iota(jnp.int32, square, 1)
    share = jnp.sum(jnp.where(diagonal, share_ref[...], 0.0), axis=1, keepdims=True)
    base = jnp.log(share) + field_ref[...]

    def back_first(c, _):
        start = pl.multiple_of(c * TILE, TILE)
        terms = split_three(cav[:, pl.ds(start, TILE)])
        out_ref[...] += join_three(jnp.dot(terms, to_slot(start), preferred_element_type=F32))
        return 0

    def back_partner(c, _):
        start = pl.multiple_of(places + pairs + c * TILE, TILE)
        terms = split_three(cav[:, pl.ds(start, TILE)])
        out_ref[...] += join_three(
            lax.dot_general(terms, from_partner(c), LAST, preferred_element_type=F32)
        )
        return 0

    half = lax.broadcasted_iota(jnp.int32, (groups // 2, 2 * cap), 1) < cap
    pl.semaphore_wait(barrier, n - 1)

    node_base = base
    weight = jnp.ones((groups, 1), F32)
    for round_index in range(ROUNDS):
        for sweep_index in range(SWEEPS):
            step = round_index * SWEEPS + sweep_index
            late = sweep_index == 0
            logit = (base if late else node_base) + totals
            logit = split_three(logit - jnp.max(logit, axis=0, keepdims=True))

            def outgoing(cols):
                at_slot = join_three(jnp.dot(logit, member[:, cols], preferred_element_type=F32))
                at_slot = at_slot - cav[:, cols]
                return jnp.exp(at_slot - jnp.max(at_slot, axis=0, keepdims=True))

            def send_part(c, _):
                start = pl.multiple_of(c * TILE, TILE)
                out = outgoing(pl.ds(start, TILE))
                out = join_three(
                    jnp.dot(split_three(out), chosen[c], preferred_element_type=F32)
                )
                for j in range(TILE // (2 * cap)):
                    x = out[:, j * 2 * cap : (j + 1) * 2 * cap]
                    r = pltpu.roll(x, cap, 1)
                    peer = c * (TILE // cap) + 2 * j
                    sbuf[step, peer] = jnp.where(half, x[: groups // 2], r[groups // 2 :])
                    sbuf[step, peer + 1] = jnp.where(half, r[: groups // 2], x[groups // 2 :])
                for j in range(group):
                    peer = c * group + j

                    @pl.when(peer != me)
                    def _():
                        pltpu.make_async_remote_copy(
                            src_ref=sbuf.at[step, peer], dst_ref=rbuf.at[step, me],
                            send_sem=send_sem.at[step], recv_sem=recv_sem.at[step, plane],
                            device_id={"node": peer}, device_id_type=pl.DeviceIdType.MESH,
                        ).start()

                return 0

            if planes <= 4:
                for k in far_first:
                    send_part(lax.rem(plane + k, planes), 0)
            else:
                lax.fori_loop(
                    0, planes,
                    lambda k, x: send_part(lax.rem(plane + planes // 2 + k, planes), x), 0,
                )

            if late:
                belief = softmax_groups(base + totals)
                mass = lax.dot_general(
                    jnp.ones((8, nodes), BF16), split_three(belief), LAST,
                    preferred_element_type=F32,
                )
                mass = mass[:, :groups] + mass[:, groups : 2 * groups] + mass[:, 2 * groups :]
                mass = jnp.concatenate([mass, jnp.zeros_like(mass)], axis=1)
                mass_out[round_index] = mass[0:1]
                mass_in[round_index, me] = mass[0:1]

                @pl.loop(1, n)
                def _(i):
                    pltpu.make_async_remote_copy(
                        src_ref=mass_out.at[round_index], dst_ref=mass_in.at[round_index, me],
                        send_sem=msend_sem.at[round_index], recv_sem=mrecv_sem.at[round_index],
                        device_id={"node": lax.rem(me + i, n)},
                        device_id_type=pl.DeviceIdType.MESH,
                    ).start()

            if step == 0:
                lax.fori_loop(0, pairs // TILE, place_pairs, 0)

            if late:
                arrived = mass_in.at[round_index, pl.ds(0, n - 1)]
                pltpu.make_async_copy(arrived, arrived, mrecv_sem.at[round_index]).wait()
                mass = loop(
                    n, lambda b, acc: acc + mass_in[round_index, b], jnp.zeros((1, 2 * cap), F32)
                )
                shift = jnp.sum(aff * mass[0:1, :groups], axis=1, keepdims=True) / every_node
                node_base = base - shift
                weight = jnp.exp(jnp.min(shift, axis=0, keepdims=True) - shift)

            def renew(cols, messages):
                messages = messages * weight
                scale = jnp.maximum(jnp.sum(messages, axis=0, keepdims=True), 1e-30)
                return group_logs(messages / scale, live[0:1, cols] > 0)

            if not late:
                weight = jnp.ones((groups, 1), F32)

            def local_part(c, acc):
                lead = pl.ds(pl.multiple_of(places + c * width, width), width)
                back = pl.ds(pl.multiple_of(places + pairs + c * width, width), width)
                lead_out, back_out = outgoing(lead), outgoing(back)
                lead_new, back_new = renew(lead, back_out), renew(back, lead_out)
                cav[:, lead] = lead_new
                cav[:, back] = back_new
                return add_up(add_up(acc, lead, lead_new), back, back_new)

            acc = loop(pairs // width, local_part, zero)

            final = step == ROUNDS * SWEEPS - 1
            if final:
                out_ref[...] = jnp.zeros_like(out_ref)
                lax.fori_loop(planes, planes + pairs // TILE, back_first, 0)
                lax.fori_loop(0, pairs // TILE, back_partner, 0)

            def take_part(offset, acc, blocks=group):
                c = lax.rem(plane - offset + planes, planes)
                arrived = rbuf.at[step, pl.ds(0, blocks)]
                pltpu.make_async_copy(arrived, arrived, recv_sem.at[step, c]).wait()
                cols = pl.ds(pl.multiple_of(c * TILE, TILE), TILE)
                tiles = []
                for j in range(group // 2):
                    peer = c * group + 2 * j
                    b0, b1 = rbuf[step, peer], rbuf[step, peer + 1]
                    top = jnp.where(half, b0, pltpu.roll(b1, cap, 1))
                    low = jnp.where(half, pltpu.roll(b0, cap, 1), b1)
                    tiles.append(jnp.concatenate([top, low], axis=0))
                fresh = renew(cols, jnp.concatenate(tiles, axis=1))
                cav[:, cols] = fresh
                if final:
                    back_first(c, 0)
                return add_up(acc, cols, fresh)

            acc = take_part(0, acc, group - 1)
            if planes <= 4:
                for k in far_first[-2::-1]:
                    acc = take_part(k, acc)
            else:
                acc = lax.fori_loop(1, planes, take_part, acc)
            totals = join_three(acc)

    marg_ref[...] = softmax_groups(node_base + totals)

    for step in range(ROUNDS * SWEEPS):
        sent = sbuf.at[step, pl.ds(0, n - 1)]
        pltpu.make_async_copy(sent, sent, send_sem.at[step]).wait()
    for round_index in range(ROUNDS):
        sent = mass_in.at[round_index, pl.ds(0, n - 1)]
        pltpu.make_async_copy(sent, sent, msend_sem.at[round_index]).wait()


def on_device(node_field, first_messages, affinity, group_share, dst_node, send_slots, source_slot):
    n = lax.axis_size("node")
    groups, nodes = node_field.shape
    slots = first_messages.shape[1]
    places = send_slots.shape[0]
    cap = places // n
    steps = ROUNDS * SWEEPS
    total = places + slots
    vmem = pl.BlockSpec(memory_space=pltpu.VMEM)
    return pl.pallas_call(
        functools.partial(kernel, n),
        out_shape=(
            jax.ShapeDtypeStruct((groups, nodes), F32),
            jax.ShapeDtypeStruct((groups, slots), F32),
        ),
        in_specs=[vmem] * 8,
        out_specs=(vmem, vmem),
        scratch_shapes=[
            pltpu.VMEM((3 * groups + 16, slots), BF16),
            pltpu.VMEM((groups, total), F32),
            pltpu.VMEM((nodes, total), BF16),
            pltpu.VMEM((8, total), jnp.int32),
            pltpu.VMEM((places // TILE, TILE, TILE), BF16),
            pltpu.VMEM((8, slots), jnp.int32),
            pltpu.VMEM((8, slots // 2), jnp.int32),
            pltpu.VMEM((steps, n, groups // 2, 2 * cap), F32),
            pltpu.VMEM((steps, n, groups // 2, 2 * cap), F32),
            pltpu.VMEM((ROUNDS, 1, 2 * cap), F32),
            pltpu.VMEM((ROUNDS, n, 1, 2 * cap), F32),
            pltpu.SemaphoreType.DMA((steps,)),
            pltpu.SemaphoreType.DMA((steps, places // TILE)),
            pltpu.SemaphoreType.DMA((ROUNDS,)),
            pltpu.SemaphoreType.DMA((ROUNDS,)),
        ],
        compiler_params=pltpu.CompilerParams(
            collective_id=0, has_side_effects=True, vmem_limit_bytes=52 * 1024 * 1024
        ),
    )(
        node_field,
        first_messages,
        affinity,
        group_share.reshape(1, groups),
        dst_node.reshape(1, slots),
        send_slots.reshape(1, places),
        send_slots.reshape(n, cap),
        source_slot.reshape(1, slots),
    )


def solution(mesh):
    split = P(None, ("parts", "node"))
    flat = P(("parts", "node"))
    return jax.shard_map(
        on_device,
        mesh=mesh,
        in_specs=(split, split, P(), P(), flat, flat, flat),
        out_specs=(split, split),
        check_vma=False,
    )
```

```python
import functools

import jax
import jax.numpy as jnp
from jax import lax
from jax.experimental import pallas as pl
from jax.experimental.pallas import tpu as pltpu
from jax.sharding import PartitionSpec as P

ROUNDS = 2
SWEEPS = 2
TILE = 256
F32 = jnp.float32
BF16 = jnp.bfloat16
LAST = (((1,), (1,)), ((), ()))


def split_three(x):
    high = x.astype(BF16)
    rest = x - high.astype(F32)
    middle = rest.astype(BF16)
    low = (rest - middle.astype(F32)).astype(BF16)
    return jnp.concatenate([high, middle, low], axis=0)


def join_three(x):
    g = x.shape[0] // 3
    return x[:g] + x[g : 2 * g] + x[2 * g :]


def softmax_groups(logits):
    weights = jnp.exp(logits - jnp.max(logits, axis=0, keepdims=True))
    return weights / jnp.sum(weights, axis=0, keepdims=True)


def loop(count, body, init):
    return lax.fori_loop(0, count, body, init, unroll=count <= 4)


def kernel(
    n, field_ref, first_ref, aff_ref, share_ref, dst_ref, send_ref, own_ref, src_ref,
    marg_ref, out_ref,
    vals, cav, member, live, chosen, pos_ref, partner, sbuf, rbuf, mass_out, mass_in,
    send_sem, recv_sem, msend_sem, mrecv_sem,
):
    me = lax.axis_index("node")
    groups, nodes = field_ref.shape
    slots = first_ref.shape[1]
    places = send_ref.shape[1]
    cap = places // n
    pairs = slots // 2
    width = 512
    planes = places // TILE
    group = TILE // cap
    plane = me // group
    far_first = sorted(range(planes), key=lambda o: (-min(o, planes - o), o))
    every_node = nodes * n

    barrier = pltpu.get_barrier_semaphore()

    @pl.loop(1, n)
    def _(i):
        pl.semaphore_signal(
            barrier, inc=1, device_id={"node": lax.rem(me + i, n)},
            device_id_type=pl.DeviceIdType.MESH,
        )

    aff = aff_ref[...]
    aff_high = aff.astype(BF16)
    aff_mid = (aff - aff_high.astype(F32)).astype(BF16)
    aff_wide = jnp.concatenate([aff_high, aff_high, aff_mid, aff_mid], axis=1)

    def group_logs(messages, alive):
        high = messages.astype(BF16)
        mid = (messages - high.astype(F32)).astype(BF16)
        stacked = jnp.concatenate([high, mid, high, mid], axis=0)
        product = jnp.dot(aff_wide, stacked, preferred_element_type=F32)
        return jnp.log(jnp.where(alive, product, 1.0))

    dst = dst_ref[...]
    src = src_ref[...]
    in_use = dst < nodes
    own = own_ref[pl.ds(me, 1), :]
    row16 = lax.broadcasted_iota(jnp.int32, (16, cap), 0)
    own_digits = jnp.where(row16 == 0, own >> 6, own & 63).astype(F32).astype(BF16)
    own_hot = jnp.where(
        lax.broadcasted_iota(jnp.int32, (cap, slots), 0) == src - (slots + me * cap), 1.0, 0.0
    ).astype(BF16)
    own_slot = jnp.dot(own_digits, own_hot, preferred_element_type=F32)
    own_slot = (own_slot[0:1] * 64.0 + own_slot[1:2]).astype(jnp.int32)
    through_own = (src >= slots + me * cap) & (src < slots + (me + 1) * cap)
    src = jnp.where(through_own, own_slot, src)
    slot_id = lax.broadcasted_iota(jnp.int32, (1, slots), 1)
    leads = in_use & (src < slots) & (src > slot_id)
    lead_f = jnp.where(leads, 1.0, 0.0)
    before = jnp.where(
        lax.broadcasted_iota(jnp.int32, (TILE, TILE), 0)
        < lax.broadcasted_iota(jnp.int32, (TILE, TILE), 1), 1.0, 0.0,
    ).astype(BF16)
    carry = jnp.zeros((1, 1), F32)
    ranks = []
    for c in range(slots // TILE):
        piece = lead_f[:, c * TILE : (c + 1) * TILE]
        inner = jnp.dot(
            jnp.broadcast_to(piece, (16, TILE)).astype(BF16), before, preferred_element_type=F32
        )[0:1]
        ranks.append(inner + carry)
        carry = carry + jnp.sum(piece, axis=1, keepdims=True)
    rank = jnp.concatenate(ranks, axis=1).astype(jnp.int32)
    position = jnp.where(
        leads, places + rank, jnp.where(in_use & (src >= slots), src - slots, -1)
    )
    pos_ref[...] = jnp.broadcast_to(position, pos_ref.shape)

    row = lax.broadcasted_iota(jnp.int32, (16, slots), 0)
    src1 = src + 1
    slot1 = slot_id + 1
    digits = jnp.where(
        row == 0, dst + 1,
        jnp.where(
            row == 1, src1 >> 6,
            jnp.where(row == 2, src1 & 63, jnp.where(row == 3, slot1 >> 6, slot1 & 63)),
        ),
    )
    vals[3 * groups :, :] = digits.astype(F32).astype(BF16)

    zero = jnp.zeros((3 * groups, nodes), F32)

    def start_logs(c, acc):
        cols = pl.ds(pl.multiple_of(c * width, width), width)
        terms = split_three(group_logs(first_ref[:, cols], dst_ref[:, cols] < nodes))
        vals[: 3 * groups, cols] = terms
        ids = lax.broadcasted_iota(jnp.int32, (nodes, width), 0)
        hot = jnp.where(ids == dst_ref[:, cols], 1.0, 0.0).astype(BF16)
        return acc + lax.dot_general(terms, hot, LAST, preferred_element_type=F32)

    totals = join_three(loop(slots // width, start_logs, zero))

    node_id = lax.broadcasted_iota(jnp.int32, (nodes, TILE), 0)

    def keep(cols, moved):
        cav[:, cols] = join_three(moved[: 3 * groups])
        node1 = moved[3 * groups : 3 * groups + 1].astype(jnp.int32)
        member[:, cols] = jnp.where(node_id + 1 == node1, 1.0, 0.0).astype(BF16)
        live[:, cols] = jnp.broadcast_to(node1, (8, TILE))

    def to_slot(start):
        ids = lax.broadcasted_iota(jnp.int32, (TILE, slots), 0) + start
        return jnp.where(ids == pos_ref[0:1, :], 1.0, 0.0).astype(BF16)

    def from_partner(c):
        cols = pl.ds(pl.multiple_of(c * TILE, TILE), TILE)
        ids = lax.broadcasted_iota(jnp.int32, (slots, TILE), 0)
        return jnp.where(ids == partner[0:1, cols], 1.0, 0.0).astype(BF16)

    def place_received(c, _):
        start = pl.multiple_of(c * TILE, TILE)
        hot = to_slot(start)
        keep(pl.ds(start, TILE), lax.dot_general(vals[...], hot, LAST, preferred_element_type=F32))
        held = lax.dot_general(hot, vals[3 * groups :, :], LAST, preferred_element_type=F32)
        held = (held[:, 3:4] * 64.0 + held[:, 4:5]).astype(jnp.int32) - 1
        chosen[c] = jnp.where(held == send_ref[:, pl.ds(start, TILE)], 1.0, 0.0).astype(BF16)
        return 0

    lax.fori_loop(0, places // TILE, place_received, 0)

    def place_pairs(c, _):
        start = pl.multiple_of(places + c * TILE, TILE)
        moved = lax.dot_general(vals[...], to_slot(start), LAST, preferred_element_type=F32)
        keep(pl.ds(start, TILE), moved)
        other = moved[3 * groups + 1 : 3 * groups + 2] * 64.0 + moved[3 * groups + 2 : 3 * groups + 3]
        cols = pl.ds(pl.multiple_of(c * TILE, TILE), TILE)
        partner[:, cols] = jnp.broadcast_to(other.astype(jnp.int32) - 1, (8, TILE))
        moved = jnp.dot(vals[...], from_partner(c), preferred_element_type=F32)
        keep(pl.ds(pl.multiple_of(start + pairs, TILE), TILE), moved)
        return 0

    for step in range(ROUNDS * SWEEPS):
        rbuf[step, me] = jnp.zeros(rbuf.shape[2:], F32)

    def add_up(acc, cols, terms):
        return acc + lax.dot_general(
            split_three(terms), member[:, cols], LAST, preferred_element_type=F32
        )

    square = (groups, groups)
    diagonal = lax.broadcasted_iota(jnp.int32, square, 0) == lax.broadcasted_iota(jnp.int32, square, 1)
    share = jnp.sum(jnp.where(diagonal, share_ref[...], 0.0), axis=1, keepdims=True)
    base = jnp.log(share) + field_ref[...]

    def back_first(c, _):
        start = pl.multiple_of(c * TILE, TILE)
        terms = split_three(cav[:, pl.ds(start, TILE)])
        out_ref[...] += join_three(jnp.dot(terms, to_slot(start), preferred_element_type=F32))
        return 0

    def back_partner(c, _):
        start = pl.multiple_of(places + pairs + c * TILE, TILE)
        terms = split_three(cav[:, pl.ds(start, TILE)])
        out_ref[...] += join_three(
            lax.dot_general(terms, from_partner(c), LAST, preferred_element_type=F32)
        )
        return 0

    half = lax.broadcasted_iota(jnp.int32, (groups // 2, 2 * cap), 1) < cap
    pl.semaphore_wait(barrier, n - 1)

    node_base = base
    weight = jnp.ones((groups, 1), F32)
    for round_index in range(ROUNDS):
        for sweep_index in range(SWEEPS):
            step = round_index * SWEEPS + sweep_index
            late = sweep_index == 0
            def send_mass():
                belief = softmax_groups(base + totals)
                mass = lax.dot_general(
                    jnp.ones((8, nodes), BF16), split_three(belief), LAST,
                    preferred_element_type=F32,
                )
                mass = mass[:, :groups] + mass[:, groups : 2 * groups] + mass[:, 2 * groups :]
                mass = jnp.concatenate([mass, jnp.zeros_like(mass)], axis=1)
                mass_out[round_index] = mass[0:1]
                mass_in[round_index, me] = mass[0:1]

                @pl.loop(1, n)
                def _(i):
                    pltpu.make_async_remote_copy(
                        src_ref=mass_out.at[round_index], dst_ref=mass_in.at[round_index, me],
                        send_sem=msend_sem.at[round_index], recv_sem=mrecv_sem.at[round_index],
                        device_id={"node": lax.rem(me + i, n)},
                        device_id_type=pl.DeviceIdType.MESH,
                    ).start()

            if late and step > 0:
                send_mass()
            logit = (base if late else node_base) + totals
            logit = split_three(logit - jnp.max(logit, axis=0, keepdims=True))

            def outgoing(cols):
                at_slot = join_three(jnp.dot(logit, member[:, cols], preferred_element_type=F32))
                at_slot = at_slot - cav[:, cols]
                return jnp.exp(at_slot - jnp.max(at_slot, axis=0, keepdims=True))

            def send_part(c, _):
                start = pl.multiple_of(c * TILE, TILE)
                out = outgoing(pl.ds(start, TILE))
                out = join_three(
                    jnp.dot(split_three(out), chosen[c], preferred_element_type=F32)
                )
                for j in range(TILE // (2 * cap)):
                    x = out[:, j * 2 * cap : (j + 1) * 2 * cap]
                    r = pltpu.roll(x, cap, 1)
                    peer = c * (TILE // cap) + 2 * j
                    sbuf[step, peer] = jnp.where(half, x[: groups // 2], r[groups // 2 :])
                    sbuf[step, peer + 1] = jnp.where(half, r[: groups // 2], x[groups // 2 :])
                for j in range(group):
                    peer = c * group + j

                    @pl.when(peer != me)
                    def _():
                        pltpu.make_async_remote_copy(
                            src_ref=sbuf.at[step, peer], dst_ref=rbuf.at[step, me],
                            send_sem=send_sem.at[step], recv_sem=recv_sem.at[step, plane],
                            device_id={"node": peer}, device_id_type=pl.DeviceIdType.MESH,
                        ).start()

                return 0

            if planes <= 4:
                for k in far_first:
                    send_part(lax.rem(plane + k, planes), 0)
            else:
                lax.fori_loop(
                    0, planes,
                    lambda k, x: send_part(lax.rem(plane + planes // 2 + k, planes), x), 0,
                )

            if step == 0:
                send_mass()
                lax.fori_loop(0, pairs // TILE, place_pairs, 0)

            if late:
                arrived = mass_in.at[round_index, pl.ds(0, n - 1)]
                pltpu.make_async_copy(arrived, arrived, mrecv_sem.at[round_index]).wait()
                mass = loop(
                    n, lambda b, acc: acc + mass_in[round_index, b], jnp.zeros((1, 2 * cap), F32)
                )
                shift = jnp.sum(aff * mass[0:1, :groups], axis=1, keepdims=True) / every_node
                node_base = base - shift
                weight = jnp.exp(jnp.min(shift, axis=0, keepdims=True) - shift)

            def renew(cols, messages):
                messages = messages * weight
                scale = jnp.maximum(jnp.sum(messages, axis=0, keepdims=True), 1e-30)
                return group_logs(messages / scale, live[0:1, cols] > 0)

            if not late:
                weight = jnp.ones((groups, 1), F32)

            def local_part(c, acc):
                lead = pl.ds(pl.multiple_of(places + c * width, width), width)
                back = pl.ds(pl.multiple_of(places + pairs + c * width, width), width)
                lead_out, back_out = outgoing(lead), outgoing(back)
                lead_new, back_new = renew(lead, back_out), renew(back, lead_out)
                cav[:, lead] = lead_new
                cav[:, back] = back_new
                return add_up(add_up(acc, lead, lead_new), back, back_new)

            acc = loop(pairs // width, local_part, zero)

            final = step == ROUNDS * SWEEPS - 1
            if final:
                out_ref[...] = jnp.zeros_like(out_ref)
                lax.fori_loop(planes, planes + pairs // TILE, back_first, 0)
                lax.fori_loop(0, pairs // TILE, back_partner, 0)

            def take_part(offset, acc, blocks=group):
                c = lax.rem(plane - offset + planes, planes)
                arrived = rbuf.at[step, pl.ds(0, blocks)]
                pltpu.make_async_copy(arrived, arrived, recv_sem.at[step, c]).wait()
                cols = pl.ds(pl.multiple_of(c * TILE, TILE), TILE)
                tiles = []
                for j in range(group // 2):
                    peer = c * group + 2 * j
                    b0, b1 = rbuf[step, peer], rbuf[step, peer + 1]
                    top = jnp.where(half, b0, pltpu.roll(b1, cap, 1))
                    low = jnp.where(half, pltpu.roll(b0, cap, 1), b1)
                    tiles.append(jnp.concatenate([top, low], axis=0))
                fresh = renew(cols, jnp.concatenate(tiles, axis=1))
                cav[:, cols] = fresh
                if final:
                    back_first(c, 0)
                return add_up(acc, cols, fresh)

            acc = take_part(0, acc, group - 1)
            if planes <= 4:
                for k in far_first[-2::-1]:
                    acc = take_part(k, acc)
            else:
                acc = lax.fori_loop(1, planes, take_part, acc)
            totals = join_three(acc)

    marg_ref[...] = softmax_groups(node_base + totals)

    for step in range(ROUNDS * SWEEPS):
        sent = sbuf.at[step, pl.ds(0, n - 1)]
        pltpu.make_async_copy(sent, sent, send_sem.at[step]).wait()
    for round_index in range(ROUNDS):
        sent = mass_in.at[round_index, pl.ds(0, n - 1)]
        pltpu.make_async_copy(sent, sent, msend_sem.at[round_index]).wait()


def on_device(node_field, first_messages, affinity, group_share, dst_node, send_slots, source_slot):
    n = lax.axis_size("node")
    groups, nodes = node_field.shape
    slots = first_messages.shape[1]
    places = send_slots.shape[0]
    cap = places // n
    steps = ROUNDS * SWEEPS
    total = places + slots
    vmem = pl.BlockSpec(memory_space=pltpu.VMEM)
    return pl.pallas_call(
        functools.partial(kernel, n),
        out_shape=(
            jax.ShapeDtypeStruct((groups, nodes), F32),
            jax.ShapeDtypeStruct((groups, slots), F32),
        ),
        in_specs=[vmem] * 8,
        out_specs=(vmem, vmem),
        scratch_shapes=[
            pltpu.VMEM((3 * groups + 16, slots), BF16),
            pltpu.VMEM((groups, total), F32),
            pltpu.VMEM((nodes, total), BF16),
            pltpu.VMEM((8, total), jnp.int32),
            pltpu.VMEM((places // TILE, TILE, TILE), BF16),
            pltpu.VMEM((8, slots), jnp.int32),
            pltpu.VMEM((8, slots // 2), jnp.int32),
            pltpu.VMEM((steps, n, groups // 2, 2 * cap), F32),
            pltpu.VMEM((steps, n, groups // 2, 2 * cap), F32),
            pltpu.VMEM((ROUNDS, 1, 2 * cap), F32),
            pltpu.VMEM((ROUNDS, n, 1, 2 * cap), F32),
            pltpu.SemaphoreType.DMA((steps,)),
            pltpu.SemaphoreType.DMA((steps, places // TILE)),
            pltpu.SemaphoreType.DMA((ROUNDS,)),
            pltpu.SemaphoreType.DMA((ROUNDS,)),
        ],
        compiler_params=pltpu.CompilerParams(
            collective_id=0, has_side_effects=True, vmem_limit_bytes=52 * 1024 * 1024
        ),
    )(
        node_field,
        first_messages,
        affinity,
        group_share.reshape(1, groups),
        dst_node.reshape(1, slots),
        send_slots.reshape(1, places),
        send_slots.reshape(n, cap),
        source_slot.reshape(1, slots),
    )


def solution(mesh):
    split = P(None, ("parts", "node"))
    flat = P(("parts", "node"))
    return jax.shard_map(
        on_device,
        mesh=mesh,
        in_specs=(split, split, P(), P(), flat, flat, flat),
        out_specs=(split, split),
        check_vma=False,
    )
```
